32 devices in a mesh: groups: 2 (over x), dp: 16 (over z, y, core).
Axes of the slice: x: 2, y: 2, z: 4, core: 2. Of those that a mesh axis runs over, the one named last changes fastest.
Arguments:
- acts: bfloat16 [5120, 8192], P(('groups', 'dp')), parts along dimension 0, may hold values from -6 to 6
- output_gradient: bfloat16 [5120, 1024], P(('groups', 'dp')), parts along dimension 0, may hold values from -6 to 6
- frozen_weight_codes: bfloat16 [8192, 1024], P('dp'), may hold values from -0.1875 to 0.1875
- weight_block_scale: float32 [64, 8], replicated, may hold values from 0.5 to 2
- adapter_down_weight: bfloat16 [16, 8192, 64], P('dp'), may hold values from -0.75 to 0.75
- adapter_up_weight: bfloat16 [16, 1024, 64], P('dp'), may hold values from -0.1875 to 0.1875
- token_adapter_index: int32 [5120, 1], P('groups'), parts along dimension 0, may hold values from 0 to 15, as said below
- adapter_position: int32 [16], replicated, may hold values from 0 to 15, each once
Outputs:
- input_gradient: bfloat16 [5120, 8192], P(('groups', 'dp')), parts along dimension 0
- down_gradient: float32 [32, 8192, 64], P(('groups', 'dp')), parts along dimension 0
- up_gradient: float32 [32, 1024, 64], P(('groups', 'dp')), parts along dimension 0
The draws below stay inside these ranges and needn't reach their ends.
There are 2 independent parts, one for each index of `groups`. The reference program is written for one: setup_inputs(seed, part) draws one part's arguments, and reference() takes and returns one part's arrays. A program takes and returns all parts, laid end to end along the dimension named above; an argument that names none is the same for every part. Nothing has to cross between parts.
Inputs may be any that keep to these rules, and one draw needn't show every extreme that they name: `token_adapter_index`: all 80 tokens of an aligned unit name one adapter. `adapter_position`: each position once.
All inputs are finite; a program needn't handle non-finite values.
Results may differ from the reference program's by a relative error of at most 0.0051.
Values may be sent and summed in bfloat16 or wider, within the bound.
A program may use at most 192 MiB of HBM per device.

```python
import math
import jax
import jax.numpy as jnp
from jax import lax

MODEL_WIDTH = 8192
VALUE_WIDTH = 1024
ADAPTER_RANK = 64
BLK = 128
SLOTS = 2
TOK_DEV = 160
ADAPTER_TOTAL = 16
TOKENS = 2560


def draw_token_adapter_index(key, part):
    key = jax.random.fold_in(key, 11)
    unit_rows = TOK_DEV // SLOTS
    unit_count = TOKENS // unit_rows
    key_len, key_step, key_first = jax.random.split(key, 3)
    lengths = jax.random.randint(key_len, (unit_count,), 1, 9).astype(jnp.int32)
    lengths = lengths.at[0].set(1)
    ends = jnp.cumsum(lengths).astype(jnp.int32)
    unit_ids = jnp.arange(unit_count, dtype=jnp.int32)
    response = jnp.sum((ends[None, :] <= unit_ids[:, None]).astype(jnp.int32), axis=1).astype(jnp.int32)
    steps_between = jax.random.randint(key_step, (unit_count,), 1, ADAPTER_TOTAL).astype(jnp.int32)
    first_adapter = jax.random.randint(key_first, (), 0, ADAPTER_TOTAL).astype(jnp.int32)
    response_adapter = ((first_adapter + jnp.cumsum(steps_between)) % ADAPTER_TOTAL).astype(jnp.int32)
    per_unit = response_adapter[response]
    return jnp.repeat(per_unit, unit_rows)[:, None].astype(jnp.int32)


def block_levels(stream_key, shape, pieces, least, largest):
    factor_of = 1.0
    for position, blocks in pieces:
        draws = jax.random.uniform(jax.random.fold_in(jax.random.fold_in(stream_key, 6), position), (blocks,), jnp.float32, least / len(pieces), largest / len(pieces))
        factor_of = factor_of * jnp.repeat(jnp.exp(draws), shape[position] // blocks).reshape((-1,) + (1,) * (len(shape) - 1 - position))
    return factor_of


def gaussian(own_key, extent, width, limit, cuts=(), kind=jnp.bfloat16):
    result = jax.random.normal(own_key, extent, jnp.float32) * width
    if len(cuts) > 0:
        result = block_levels(own_key, extent, cuts, -0.22, 0.18) * result
    return jnp.clip(result, min=-limit, max=limit).astype(kind)


def setup_inputs(seed: int = 0, part: int = 0) -> dict:
    splits = jax.random.split(jax.random.key(seed), 9)
    part_keys = jax.random.split(jax.random.fold_in(splits[8], part), 9)
    acts = gaussian(part_keys[0], (TOKENS, MODEL_WIDTH), 1.0, 6.0, ((0, 16),))
    output_gradient = gaussian(part_keys[1], (TOKENS, VALUE_WIDTH), 1.0, 6.0, ((0, 16),))
    frozen_weight_codes = gaussian(splits[2], (MODEL_WIDTH, VALUE_WIDTH), VALUE_WIDTH ** -0.5, 0.1875, ((0, 16),))
    weight_block_scale = jnp.clip(jnp.exp(jax.random.uniform(splits[3], (MODEL_WIDTH // BLK, VALUE_WIDTH // BLK), jnp.float32, math.log(0.5), math.log(2.0))), 0.5, 2.0)
    adapter_down_weight = gaussian(splits[4], (ADAPTER_TOTAL, MODEL_WIDTH, ADAPTER_RANK), ADAPTER_RANK ** -0.5, 0.75, ((0, 16),))
    adapter_up_weight = gaussian(splits[5], (ADAPTER_TOTAL, VALUE_WIDTH, ADAPTER_RANK), VALUE_WIDTH ** -0.5, 0.1875, ((0, 16),))
    token_adapter_index = draw_token_adapter_index(jax.random.fold_in(jax.random.fold_in(splits[8], part), 71), part)
    adapter_position = jax.random.permutation(splits[7], ADAPTER_TOTAL).astype(jnp.int32)
    return dict(acts=acts, output_gradient=output_gradient, frozen_weight_codes=frozen_weight_codes, weight_block_scale=weight_block_scale, adapter_down_weight=adapter_down_weight, adapter_up_weight=adapter_up_weight, token_adapter_index=token_adapter_index, adapter_position=adapter_position)


def reference(acts, output_gradient, frozen_weight_codes, weight_block_scale, adapter_down_weight, adapter_up_weight, token_adapter_index, adapter_position):
    scales = jnp.repeat(jnp.repeat(weight_block_scale, BLK, axis=0), BLK, axis=1)
    weight = (frozen_weight_codes.astype(jnp.float32) * scales).astype(jnp.bfloat16)
    frozen_gradient = jnp.dot(output_gradient, weight.T, preferred_element_type=jnp.float32)
    unit_rows = TOK_DEV // SLOTS
    unit_count = TOKENS // unit_rows
    unit_place = adapter_position[token_adapter_index[::unit_rows, 0]].astype(jnp.int32)
    unit_acts = acts.reshape(unit_count, unit_rows, MODEL_WIDTH)
    member_gradients = output_gradient.reshape(unit_count, unit_rows, VALUE_WIDTH)

    def advance(totals, inputs_now):
        sum_down, sum_up = totals
        rows_x, rows_g, stored_position = inputs_now
        down_matrix = lax.dynamic_index_in_dim(adapter_down_weight, stored_position, 0, keepdims=False)
        up_matrix = lax.dynamic_index_in_dim(adapter_up_weight, stored_position, 0, keepdims=False)
        low_terms = jnp.dot(rows_g, up_matrix, preferred_element_type=jnp.float32).astype(jnp.bfloat16)
        projected_rows = jnp.dot(rows_x, down_matrix, preferred_element_type=jnp.float32).astype(jnp.bfloat16)
        back_rows = (0.5 * jnp.dot(low_terms, down_matrix.T, preferred_element_type=jnp.float32)).astype(jnp.bfloat16)
        part_down = 0.5 * jnp.dot(rows_x.T, low_terms, preferred_element_type=jnp.float32)
        part_up = 0.5 * jnp.dot(rows_g.T, projected_rows, preferred_element_type=jnp.float32)
        sum_down = sum_down.at[stored_position].add(part_down)
        sum_up = sum_up.at[stored_position].add(part_up)
        return (sum_down, sum_up), back_rows

    start_down = jnp.zeros((ADAPTER_TOTAL, MODEL_WIDTH, ADAPTER_RANK), jnp.float32)
    start_up = jnp.zeros((ADAPTER_TOTAL, VALUE_WIDTH, ADAPTER_RANK), jnp.float32)
    (down_gradient, up_gradient), backs = lax.scan(advance, (start_down, start_up), (unit_acts, member_gradients, unit_place))
    input_gradient = (frozen_gradient + backs.reshape(TOKENS, MODEL_WIDTH).astype(jnp.float32)).astype(jnp.bfloat16)
    return input_gradient, down_gradient, up_gradient
```

```python
import functools

import jax
import jax.numpy as jnp
from jax import lax
from jax.experimental import pallas as pl
from jax.experimental.pallas import tpu as pltpu
from jax.sharding import PartitionSpec as P

BLK = 128
SLOTS = 2
NT = (((1,), (1,)), ((), ()))
TN = (((0,), (0,)), ((), ()))
F32 = jnp.float32
BF16 = jnp.bfloat16


def slab_kernel(unit_rows, place, grads, acts, weight, up, down, out, proj, summed):
    step = pl.program_id(0)

    @pl.when(step == 0)
    def _():
        summed[...] = jnp.zeros_like(summed)

    base = lax.dot_general(grads[...], weight[...], NT, preferred_element_type=F32)
    units = grads.shape[0] // unit_rows
    for u in range(units):
        rows = pl.ds(u * unit_rows, unit_rows)
        p = place[step * units + u]
        down_p = down[p]
        x = acts[rows, :]
        low = lax.dot_general(grads[rows, :], up[p], NT, preferred_element_type=F32).astype(BF16)
        proj[rows, :] = lax.dot_general(x, down_p, NT, preferred_element_type=F32)
        back = (0.5 * jnp.dot(low, down_p, preferred_element_type=F32)).astype(BF16)
        here = base[u * unit_rows : (u + 1) * unit_rows, :]
        out[rows, :] = (here + back.astype(F32)).astype(BF16)
        summed[p] += 0.5 * lax.dot_general(low, x, TN, preferred_element_type=F32)


def up_kernel(place_ref, me_ref, grads, proj, total):
    step = pl.program_id(0)
    unit_rows = grads.shape[0]

    @pl.when(step == 0)
    def _():
        total[...] = jnp.zeros_like(total)

    @pl.when(place_ref[step] == me_ref[0])
    def _():
        total[...] += 0.5 * lax.dot_general(
            proj[...], grads[...], TN, preferred_element_type=F32
        )


def shards(
    acts,
    output_gradient,
    frozen_weight_codes,
    weight_block_scale,
    adapter_down_weight,
    adapter_up_weight,
    token_adapter_index,
    adapter_position,
):
    token_rows, row_extent = acts.shape
    out_width = output_gradient.shape[1]
    rank = adapter_down_weight.shape[2]
    n = lax.axis_size("dp")
    me = lax.axis_index("dp")
    unit_rows = token_rows // SLOTS
    slab = row_extent // n
    tokens = token_rows * n
    unit_place = adapter_position[token_adapter_index[::unit_rows, 0]]

    grads_all = lax.all_gather(output_gradient, "dp", axis=0, tiled=True)
    up_all = lax.all_gather(adapter_up_weight.transpose(0, 2, 1), "dp", axis=0, tiled=True)
    down_slabs = lax.all_to_all(
        adapter_down_weight.transpose(0, 2, 1), "dp", split_axis=2, concat_axis=0, tiled=True
    )
    acts_slab = lax.all_to_all(acts, "dp", split_axis=1, concat_axis=0, tiled=True)

    row_ids = me * slab + jnp.arange(slab, dtype=jnp.int32)
    scale_rows = weight_block_scale[row_ids // BLK]
    codes = frozen_weight_codes.astype(F32).reshape(slab, out_width // BLK, BLK)
    weight = (codes * scale_rows[:, :, None]).astype(BF16).reshape(slab, out_width)

    adapters = up_all.shape[0]
    rows = 2 * token_rows
    whole = lambda *shape: pl.BlockSpec(shape, lambda i, place: (0,) * len(shape))
    out, proj_part, summed = pl.pallas_call(
        functools.partial(slab_kernel, unit_rows),
        grid_spec=pltpu.PrefetchScalarGridSpec(
            num_scalar_prefetch=1,
            grid=(tokens // rows,),
            in_specs=[
                pl.BlockSpec((rows, out_width), lambda i, place: (i, 0)),
                pl.BlockSpec((rows, slab), lambda i, place: (i, 0)),
                whole(slab, out_width),
                whole(adapters, rank, out_width),
                whole(adapters, rank, slab),
            ],
            out_specs=[
                pl.BlockSpec((rows, slab), lambda i, place: (i, 0)),
                pl.BlockSpec((rows, rank), lambda i, place: (i, 0)),
                whole(adapters, rank, slab),
            ],
        ),
        out_shape=[
            jax.ShapeDtypeStruct((tokens, slab), BF16),
            jax.ShapeDtypeStruct((tokens, rank), F32),
            jax.ShapeDtypeStruct((adapters, rank, slab), F32),
        ],
        compiler_params=pltpu.CompilerParams(vmem_limit_bytes=56 * 2**20),
    )(unit_place, grads_all, acts_slab, weight, up_all, down_slabs)

    proj_own = lax.psum_scatter(proj_part, "dp", scatter_dimension=0, tiled=True).astype(BF16)
    proj_all = lax.all_gather(proj_own, "dp", axis=0, tiled=True)
    input_gradient = lax.all_to_all(out, "dp", split_axis=0, concat_axis=1, tiled=True)
    down_gradient = lax.all_to_all(
        summed.astype(BF16), "dp", split_axis=0, concat_axis=2, tiled=True
    ).astype(F32)
    up_gradient = pl.pallas_call(
        up_kernel,
        grid_spec=pltpu.PrefetchScalarGridSpec(
            num_scalar_prefetch=2,
            grid=(tokens // unit_rows,),
            in_specs=[
                pl.BlockSpec((unit_rows, out_width), lambda i, place, me: (i, 0)),
                pl.BlockSpec((unit_rows, rank), lambda i, place, me: (i, 0)),
            ],
            out_specs=pl.BlockSpec((rank, out_width), lambda i, place, me: (0, 0)),
        ),
        out_shape=jax.ShapeDtypeStruct((rank, out_width), F32),
    )(unit_place, me.astype(jnp.int32).reshape(1), grads_all, proj_all)
    return (
        input_gradient,
        down_gradient.transpose(0, 2, 1),
        up_gradient[None].transpose(0, 2, 1),
    )


def solution(mesh):
    placed = (
        P(("groups", "dp"), None),
        P(("groups", "dp"), None),
        P("dp", None),
        P(),
        P("dp", None, None),
        P("dp", None, None),
        P("groups", None),
        P(),
    )
    return jax.shard_map(
        shards,
        mesh=mesh,
        in_specs=placed,
        out_specs=(
            P(("groups", "dp"), None),
            P(("groups", "dp"), None, None),
            P(("groups", "dp"), None, None),
        ),
        check_vma=False,
    )
```

```python
import functools

import jax
import jax.numpy as jnp
from jax import lax
from jax.experimental import pallas as pl
from jax.experimental.pallas import tpu as pltpu
from jax.sharding import PartitionSpec as P

BLK = 128
SLOTS = 2
NT = (((1,), (1,)), ((), ()))
TN = (((0,), (0,)), ((), ()))
F32 = jnp.float32
BF16 = jnp.bfloat16


def slab_kernel(unit_rows, place, grads, acts, weight, up, down, out, proj, summed):
    step = pl.program_id(0)

    @pl.when(step == 0)
    def _():
        summed[...] = jnp.zeros_like(summed)

    base = lax.dot_general(grads[...], weight[...], NT, preferred_element_type=F32)
    units = grads.shape[0] // unit_rows
    for u in range(units):
        rows = pl.ds(u * unit_rows, unit_rows)
        p = place[step * units + u]
        down_p = down[p]
        x = acts[rows, :]
        low = lax.dot_general(grads[rows, :], up[p], NT, preferred_element_type=F32).astype(BF16)
        proj[rows, :] = lax.dot_general(x, down_p, NT, preferred_element_type=F32)
        back = (0.5 * jnp.dot(low, down_p, preferred_element_type=F32)).astype(BF16)
        here = base[u * unit_rows : (u + 1) * unit_rows, :]
        out[rows, :] = (here + back.astype(F32)).astype(BF16)
        summed[p] += 0.5 * lax.dot_general(low, x, TN, preferred_element_type=F32)


def up_kernel(place_ref, me_ref, grads, proj, total):
    step = pl.program_id(0)
    unit_rows = grads.shape[0]

    @pl.when(step == 0)
    def _():
        total[...] = jnp.zeros_like(total)

    @pl.when(place_ref[step] == me_ref[0])
    def _():
        total[...] += 0.5 * lax.dot_general(
            proj[...], grads[...], TN, preferred_element_type=F32
        )


def fused_kernel(n, unit_rows, place, acts, grads, weight, up, down, out, dgrad, ugrad,
                 part, part_in, own, projs, stage, landed, spread, dsend, dland,
                 part_s, part_r, proj_s, proj_r, out_s, out_r, down_s, down_r):
    me = lax.axis_index("dp")
    rows = SLOTS * unit_rows
    slab = weight.shape[0]
    rank = down.shape[1]
    wide = SLOTS * rank

    def peer(s):
        return lax.rem(me + s, n)

    def send(src, dst, send_sem, recv_sem, j):
        return pltpu.make_async_remote_copy(
            src_ref=src, dst_ref=dst, send_sem=send_sem.at[j], recv_sem=recv_sem.at[me],
            device_id={"dp": j}, device_id_type=pl.DeviceIdType.MESH)

    def arrival(src, dst, send_sem, recv_sem, j):
        return pltpu.make_async_remote_copy(
            src_ref=src, dst_ref=dst, send_sem=send_sem.at[j], recv_sem=recv_sem.at[j],
            device_id={"dp": j}, device_id_type=pl.DeviceIdType.MESH)

    barrier = pltpu.get_barrier_semaphore()

    @pl.loop(1, n)
    def _(s):
        pl.semaphore_signal(barrier, inc=1, device_id={"dp": peer(s)},
                            device_id_type=pl.DeviceIdType.MESH)

    pl.semaphore_wait(barrier, n - 1)

    def tile(j, u):
        return pl.ds(pl.multiple_of(j * rows + u * unit_rows, 16), unit_rows)

    def project(j, dst):
        both = [
            lax.dot_general(acts[tile(j, u), :], down[place[SLOTS * j + u]], NT,
                            preferred_element_type=F32)
            for u in range(SLOTS)
        ]
        dst[j] = jnp.concatenate(both, axis=1)

    @pl.loop(1, n)
    def _(s):
        j = peer(s)
        project(j, part)
        send(part.at[j], part_in.at[me], part_s, part_r, j).start()

    project(me, part_in)

    lane_half = lax.broadcasted_iota(jnp.int32, (unit_rows, 2 * rank), 1) // rank

    def block(j, dst):
        for u in range(SLOTS):
            at = tile(j, u)
            p = place[SLOTS * j + u]
            g = grads[at, :]
            low = lax.dot_general(g, up[p], NT, preferred_element_type=F32).astype(BF16)
            base = lax.dot_general(g, weight[...], NT, preferred_element_type=F32)
            back = (0.5 * jnp.dot(low, down[p], preferred_element_type=F32)).astype(BF16)
            dst[j, pl.ds(u * unit_rows, unit_rows), :] = (base + back.astype(F32)).astype(BF16)
            low = low.astype(F32)
            twice = jnp.concatenate([low, low], axis=1)
            for c in range(n // 2):
                kept = jnp.where(lane_half + 2 * c == p, twice, 0.0)
                spread[at, pl.ds(c * 2 * rank, 2 * rank)] = kept.astype(BF16)

    @pl.loop(1, n)
    def _(s):
        j = peer(s)
        block(j, stage)
        send(stage.at[j], landed.at[me], out_s, out_r, j).start()

    block(me, landed)

    @pl.loop(1, n)
    def _(s):
        j = peer(s)
        arrival(part.at[j], part_in.at[j], part_s, part_r, j).wait()

    total = part_in[0]
    for j in range(1, n):
        total = total + part_in[j]
    own[...] = total.astype(BF16)

    @pl.loop(1, n)
    def _(s):
        j = peer(s)
        send(own, projs.at[me], proj_s, proj_r, j).start()

    projs[me] = own[...]

    group = 4

    @pl.loop(0, n // group)
    def _(c):
        cols = pl.ds(pl.multiple_of(c * group * rank, group * rank), group * rank)
        got = 0.5 * lax.dot_general(spread[:, cols], acts[...], TN, preferred_element_type=F32)
        for i in range(group):
            dsend[c * group + i] = got[i * rank : (i + 1) * rank, :].astype(BF16)
        for i in range(group):
            j = c * group + i

            @pl.when(j != me)
            def _():
                send(dsend.at[j], dland.at[me], down_s, down_r, j).start()

    dland[me] = dsend[me]

    @pl.loop(1, n)
    def _(s):
        j = peer(s)
        arrival(own, projs.at[j], proj_s, proj_r, j).wait()

    ugrad[...] = jnp.zeros_like(ugrad)

    @pl.loop(0, n)
    def _(j):
        both = projs[j].astype(F32)
        for u in range(SLOTS):
            keep = jnp.where(place[SLOTS * j + u] == me, 0.5, 0.0)
            mine = (both[:, u * rank : (u + 1) * rank] * keep).astype(BF16)
            ugrad[...] += lax.dot_general(mine, grads[tile(j, u), :], TN,
                                          preferred_element_type=F32)

    def place_out(j):
        cols = pl.ds(pl.multiple_of(j * slab, slab), slab)
        out[:, cols] = landed[j]

    def place_down(j):
        cols = pl.ds(pl.multiple_of(j * slab, slab), slab)
        dgrad[:, cols] = dland[j].astype(F32)

    place_out(me)
    place_down(me)

    @pl.loop(1, n)
    def _(s):
        j = lax.rem(me + n - s, n)
        arrival(stage.at[j], landed.at[j], out_s, out_r, j).wait()
        place_out(j)

    @pl.loop(1, n)
    def _(s):
        j = lax.rem(me + n - s, n)
        arrival(dsend.at[j], dland.at[j], down_s, down_r, j).wait()
        place_down(j)


def fused(n, unit_place, acts_slab, grads_all, weight, up_all, down_slabs):
    tokens, slab = acts_slab.shape
    out_width = grads_all.shape[1]
    rank = up_all.shape[1]
    rows = tokens // n
    unit_rows = rows // SLOTS
    vmem = pl.BlockSpec(memory_space=pltpu.VMEM)
    dma = pltpu.SemaphoreType.DMA((n,))
    return pl.pallas_call(
        functools.partial(fused_kernel, n, unit_rows),
        in_specs=[pl.BlockSpec(memory_space=pltpu.SMEM)] + [vmem] * 5,
        out_specs=[vmem] * 3,
        out_shape=[
            jax.ShapeDtypeStruct((rows, n * slab), BF16),
            jax.ShapeDtypeStruct((rank, n * slab), F32),
            jax.ShapeDtypeStruct((rank, out_width), F32),
        ],
        scratch_shapes=[
            pltpu.VMEM((n, unit_rows, SLOTS * rank), F32),
            pltpu.VMEM((n, unit_rows, SLOTS * rank), F32),
            pltpu.VMEM((unit_rows, SLOTS * rank), BF16),
            pltpu.VMEM((n, unit_rows, SLOTS * rank), BF16),
            pltpu.VMEM((n, rows, slab), BF16),
            pltpu.VMEM((n, rows, slab), BF16),
            pltpu.VMEM((tokens, n * rank), BF16),
            pltpu.VMEM((n, rank, slab), BF16),
            pltpu.VMEM((n, rank, slab), BF16),
        ] + [dma] * 8,
        compiler_params=pltpu.CompilerParams(
            collective_id=0, has_side_effects=True, vmem_limit_bytes=52 * 2**20),
        cost_estimate=pl.CostEstimate(
            flops=2 * tokens * slab * out_width * 4, bytes_accessed=30 * 2**20, transcendentals=0),
    )(unit_place, acts_slab, grads_all, weight, up_all, down_slabs)


def shards(
    acts,
    output_gradient,
    frozen_weight_codes,
    weight_block_scale,
    adapter_down_weight,
    adapter_up_weight,
    token_adapter_index,
    adapter_position,
):
    token_rows, row_extent = acts.shape
    out_width = output_gradient.shape[1]
    rank = adapter_down_weight.shape[2]
    n = lax.axis_size("dp")
    me = lax.axis_index("dp")
    unit_rows = token_rows // SLOTS
    slab = row_extent // n
    tokens = token_rows * n
    unit_adapter = token_adapter_index.reshape(-1, unit_rows)[:, :1]
    every = jnp.arange(adapter_position.shape[0], dtype=jnp.int32)[None, :]
    unit_place = jnp.sum(jnp.where(unit_adapter == every, adapter_position[None, :], 0), axis=1)

    grads_all = lax.all_gather(output_gradient, "dp", axis=0, tiled=True)
    up_all = lax.all_gather(adapter_up_weight.transpose(0, 2, 1), "dp", axis=0, tiled=True)
    down_slabs = lax.all_to_all(
        adapter_down_weight.transpose(0, 2, 1), "dp", split_axis=2, concat_axis=0, tiled=True
    )
    acts_slab = lax.all_to_all(acts, "dp", split_axis=1, concat_axis=0, tiled=True)

    row_ids = me * slab + jnp.arange(slab, dtype=jnp.int32)
    scale_rows = weight_block_scale[row_ids // BLK]
    codes = frozen_weight_codes.astype(F32).reshape(slab, out_width // BLK, BLK)
    weight = (codes * scale_rows[:, :, None]).astype(BF16).reshape(slab, out_width)

    adapters = up_all.shape[0]
    if grads_all.size <= 4 * 2**20 and slab % BLK == 0 and adapters == n:
        input_gradient, down_t, up_t = fused(
            n, unit_place, acts_slab, grads_all, weight, up_all, down_slabs)
        return (
            input_gradient,
            down_t[None].transpose(0, 2, 1),
            up_t[None].transpose(0, 2, 1),
        )
    rows = 2 * token_rows
    whole = lambda *shape: pl.BlockSpec(shape, lambda i, place: (0,) * len(shape))
    out, proj_part, summed = pl.pallas_call(
        functools.partial(slab_kernel, unit_rows),
        grid_spec=pltpu.PrefetchScalarGridSpec(
            num_scalar_prefetch=1,
            grid=(tokens // rows,),
            in_specs=[
                pl.BlockSpec((rows, out_width), lambda i, place: (i, 0)),
                pl.BlockSpec((rows, slab), lambda i, place: (i, 0)),
                whole(slab, out_width),
                whole(adapters, rank, out_width),
                whole(adapters, rank, slab),
            ],
            out_specs=[
                pl.BlockSpec((rows, slab), lambda i, place: (i, 0)),
                pl.BlockSpec((rows, rank), lambda i, place: (i, 0)),
                whole(adapters, rank, slab),
            ],
        ),
        out_shape=[
            jax.ShapeDtypeStruct((tokens, slab), BF16),
            jax.ShapeDtypeStruct((tokens, rank), F32),
            jax.ShapeDtypeStruct((adapters, rank, slab), F32),
        ],
        compiler_params=pltpu.CompilerParams(vmem_limit_bytes=56 * 2**20),
    )(unit_place, grads_all, acts_slab, weight, up_all, down_slabs)

    proj_own = lax.psum_scatter(proj_part, "dp", scatter_dimension=0, tiled=True).astype(BF16)
    proj_all = lax.all_gather(proj_own, "dp", axis=0, tiled=True)
    input_gradient = lax.all_to_all(out, "dp", split_axis=0, concat_axis=1, tiled=True)
    down_gradient = lax.all_to_all(
        summed.astype(BF16), "dp", split_axis=0, concat_axis=2, tiled=True
    ).astype(F32)
    up_gradient = pl.pallas_call(
        up_kernel,
        grid_spec=pltpu.PrefetchScalarGridSpec(
            num_scalar_prefetch=2,
            grid=(tokens // unit_rows,),
            in_specs=[
                pl.BlockSpec((unit_rows, out_width), lambda i, place, me: (i, 0)),
                pl.BlockSpec((unit_rows, rank), lambda i, place, me: (i, 0)),
            ],
            out_specs=pl.BlockSpec((rank, out_width), lambda i, place, me: (0, 0)),
        ),
        out_shape=jax.ShapeDtypeStruct((rank, out_width), F32),
    )(unit_place, me.astype(jnp.int32).reshape(1), grads_all, proj_all)
    return (
        input_gradient,
        down_gradient.transpose(0, 2, 1),
        up_gradient[None].transpose(0, 2, 1),
    )


def solution(mesh):
    placed = (
        P(("groups", "dp"), None),
        P(("groups", "dp"), None),
        P("dp", None),
        P(),
        P("dp", None, None),
        P("dp", None, None),
        P("groups", None),
        P(),
    )
    return jax.shard_map(
        shards,
        mesh=mesh,
        in_specs=placed,
        out_specs=(
            P(("groups", "dp"), None),
            P(("groups", "dp"), None, None),
            P(("groups", "dp"), None, None),
        ),
        check_vma=False,
    )
```

```python
import functools

import jax
import jax.numpy as jnp
from jax import lax
from jax.experimental import pallas as pl
from jax.experimental.pallas import tpu as pltpu
from jax.sharding import PartitionSpec as P

BLK = 128
SLOTS = 2
NT = (((1,), (1,)), ((), ()))
TN = (((0,), (0,)), ((), ()))
F32 = jnp.float32
BF16 = jnp.bfloat16


def slab_kernel(unit_rows, place, grads, acts, weight, up, down, out, proj, summed):
    step = pl.program_id(0)

    @pl.when(step == 0)
    def _():
        summed[...] = jnp.zeros_like(summed)

    base = lax.dot_general(grads[...], weight[...], NT, preferred_element_type=F32)
    units = grads.shape[0] // unit_rows
    for u in range(units):
        rows = pl.ds(u * unit_rows, unit_rows)
        p = place[step * units + u]
        down_p = down[p]
        x = acts[rows, :]
        low = lax.dot_general(grads[rows, :], up[p], NT, preferred_element_type=F32).astype(BF16)
        proj[rows, :] = lax.dot_general(x, down_p, NT, preferred_element_type=F32)
        back = (0.5 * jnp.dot(low, down_p, preferred_element_type=F32)).astype(BF16)
        here = base[u * unit_rows : (u + 1) * unit_rows, :]
        out[rows, :] = (here + back.astype(F32)).astype(BF16)
        summed[p] += 0.5 * lax.dot_general(low, x, TN, preferred_element_type=F32)


def up_kernel(place_ref, me_ref, grads, proj, total):
    step = pl.program_id(0)
    unit_rows = grads.shape[0]

    @pl.when(step == 0)
    def _():
        total[...] = jnp.zeros_like(total)

    @pl.when(place_ref[step] == me_ref[0])
    def _():
        total[...] += 0.5 * lax.dot_general(
            proj[...], grads[...], TN, preferred_element_type=F32
        )


def exchange_kernel(n, acts, down, acts_out, down_out, acts_s, acts_r, down_s, down_r, local):
    me = lax.axis_index("dp")
    rows = acts.shape[0]
    slab = acts.shape[1] // n

    def peer(s):
        return lax.rem(me + s, n)

    def cols(j):
        return pl.ds(pl.multiple_of(j * slab, slab), slab)

    def lines(j):
        return pl.ds(pl.multiple_of(j * rows, 16), rows)

    def remote(src, dst, send_sem, recv_sem, j):
        return pltpu.make_async_remote_copy(
            src_ref=src, dst_ref=dst, send_sem=send_sem, recv_sem=recv_sem,
            device_id={"dp": j}, device_id_type=pl.DeviceIdType.MESH)

    mine = pltpu.make_async_copy(acts.at[:, cols(me)], acts_out.at[lines(me), :], local.at[0])
    own = pltpu.make_async_copy(down.at[:, cols(me)], down_out.at[me], local.at[1])
    mine.start()
    own.start()
    barrier = pltpu.get_barrier_semaphore()

    @pl.loop(1, n)
    def _(s):
        pl.semaphore_signal(barrier, inc=1, device_id={"dp": peer(s)},
                            device_id_type=pl.DeviceIdType.MESH)

    pl.semaphore_wait(barrier, n - 1)

    @pl.loop(1, n)
    def _(s):
        j = peer(s)
        remote(down.at[:, cols(j)], down_out.at[me], down_s.at[j], down_r.at[me], j).start()
        remote(acts.at[:, cols(j)], acts_out.at[lines(me), :], acts_s.at[j], acts_r.at[me],
               j).start()

    mine.wait()
    own.wait()

    @pl.loop(1, n)
    def _(s):
        j = lax.rem(me + n - s, n)
        remote(down.at[:, cols(j)], down_out.at[j], down_s.at[j], down_r.at[j], j).wait()
        remote(acts.at[:, cols(j)], acts_out.at[lines(j), :], acts_s.at[j], acts_r.at[j],
               j).wait()


def exchange(n, acts, down_t):
    rows, width = acts.shape
    slab = width // n
    dma = pltpu.SemaphoreType.DMA((n,))
    anywhere = pl.BlockSpec(memory_space=pl.ANY)
    return pl.pallas_call(
        functools.partial(exchange_kernel, n),
        in_specs=[anywhere] * 2,
        out_specs=[anywhere] * 2,
        out_shape=[
            jax.ShapeDtypeStruct((n * rows, slab), BF16),
            jax.ShapeDtypeStruct((n, down_t.shape[0], slab), BF16),
        ],
        scratch_shapes=[dma] * 4 + [pltpu.SemaphoreType.DMA((2,))],
        compiler_params=pltpu.CompilerParams(collective_id=1, has_side_effects=True),
        cost_estimate=pl.CostEstimate(
            flops=0, bytes_accessed=200 * 2**20, transcendentals=0),
    )(acts, down_t)


def fused_kernel(n, unit_rows, place, acts, both_all, weight, down, out, dgrad, ugrad,
                 part, part_in, own, projs, stage, landed, spread, dsend, dland,
                 part_s, part_r, proj_s, proj_r, out_s, out_r, down_s, down_r):
    me = lax.axis_index("dp")
    rows = SLOTS * unit_rows
    slab = weight.shape[0]
    rank = down.shape[1]
    wide = SLOTS * rank

    def peer(s):
        return lax.rem(me + s, n)

    def send(src, dst, send_sem, recv_sem, j):
        return pltpu.make_async_remote_copy(
            src_ref=src, dst_ref=dst, send_sem=send_sem.at[j], recv_sem=recv_sem.at[me],
            device_id={"dp": j}, device_id_type=pl.DeviceIdType.MESH)

    def arrival(src, dst, send_sem, recv_sem, j):
        return pltpu.make_async_remote_copy(
            src_ref=src, dst_ref=dst, send_sem=send_sem.at[j], recv_sem=recv_sem.at[j],
            device_id={"dp": j}, device_id_type=pl.DeviceIdType.MESH)

    barrier = pltpu.get_barrier_semaphore()

    @pl.loop(1, n)
    def _(s):
        pl.semaphore_signal(barrier, inc=1, device_id={"dp": peer(s)},
                            device_id_type=pl.DeviceIdType.MESH)

    pl.semaphore_wait(barrier, n - 1)

    def grad_tile(j, u):
        return both_all[j, pl.ds(u * unit_rows, unit_rows), :]

    def up_of(p):
        return both_all[p, pl.ds(rows, rank), :]

    def tile(j, u):
        return pl.ds(pl.multiple_of(j * rows + u * unit_rows, 16), unit_rows)

    def project(j, dst):
        both = [
            lax.dot_general(acts[tile(j, u), :], down[place[SLOTS * j + u]], NT,
                            preferred_element_type=F32)
            for u in range(SLOTS)
        ]
        dst[j] = jnp.concatenate(both, axis=1).astype(BF16)

    @pl.loop(1, n)
    def _(s):
        j = peer(s)
        project(j, part)
        send(part.at[j], part_in.at[me], part_s, part_r, j).start()

    project(me, part_in)

    lane_half = lax.broadcasted_iota(jnp.int32, (unit_rows, 2 * rank), 1) // rank

    def block(j, dst):
        for u in range(SLOTS):
            at = tile(j, u)
            p = place[SLOTS * j + u]
            g = grad_tile(j, u)
            low = lax.dot_general(g, up_of(p), NT, preferred_element_type=F32).astype(BF16)
            base = lax.dot_general(g, weight[...], NT, preferred_element_type=F32)
            back = (0.5 * jnp.dot(low, down[p], preferred_element_type=F32)).astype(BF16)
            dst[j, pl.ds(u * unit_rows, unit_rows), :] = (base + back.astype(F32)).astype(BF16)
            low = low.astype(F32)
            twice = jnp.concatenate([low, low], axis=1)
            for c in range(n // 2):
                kept = jnp.where(lane_half + 2 * c == p, twice, 0.0)
                spread[at, pl.ds(c * 2 * rank, 2 * rank)] = kept.astype(BF16)

    @pl.loop(1, n)
    def _(s):
        j = peer(s)
        block(j, stage)
        send(stage.at[j], landed.at[me], out_s, out_r, j).start()

    block(me, landed)

    @pl.loop(1, n)
    def _(s):
        j = peer(s)
        arrival(part.at[j], part_in.at[j], part_s, part_r, j).wait()

    total = part_in[0].astype(F32)
    for j in range(1, n):
        total = total + part_in[j].astype(F32)
    own[...] = total.astype(BF16)

    @pl.loop(1, n)
    def _(s):
        j = peer(s)
        send(own, projs.at[me], proj_s, proj_r, j).start()

    projs[me] = own[...]

    group = 4

    @pl.loop(0, n // group)
    def _(c):
        cols = pl.ds(pl.multiple_of(c * group * rank, group * rank), group * rank)
        got = 0.5 * lax.dot_general(spread[:, cols], acts[...], TN, preferred_element_type=F32)
        for i in range(group):
            dsend[c * group + i] = got[i * rank : (i + 1) * rank, :].astype(BF16)
        for i in range(group):
            j = c * group + i

            @pl.when(j != me)
            def _():
                send(dsend.at[j], dland.at[me], down_s, down_r, j).start()

    dland[me] = dsend[me]

    @pl.loop(1, n)
    def _(s):
        j = peer(s)
        arrival(own, projs.at[j], proj_s, proj_r, j).wait()

    ugrad[...] = jnp.zeros_like(ugrad)

    @pl.loop(0, n)
    def _(j):
        both = projs[j].astype(F32)
        for u in range(SLOTS):
            keep = jnp.where(place[SLOTS * j + u] == me, 0.5, 0.0)
            mine = (both[:, u * rank : (u + 1) * rank] * keep).astype(BF16)
            ugrad[...] += lax.dot_general(mine, grad_tile(j, u), TN,
                                          preferred_element_type=F32)

    def place_out(j):
        cols = pl.ds(pl.multiple_of(j * slab, slab), slab)
        out[:, cols] = landed[j]

    def place_down(j):
        cols = pl.ds(pl.multiple_of(j * slab, slab), slab)
        dgrad[:, cols] = dland[j].astype(F32)

    place_out(me)
    place_down(me)

    @pl.loop(1, n)
    def _(s):
        j = lax.rem(me + n - s, n)
        arrival(stage.at[j], landed.at[j], out_s, out_r, j).wait()
        place_out(j)

    @pl.loop(1, n)
    def _(s):
        j = lax.rem(me + n - s, n)
        arrival(dsend.at[j], dland.at[j], down_s, down_r, j).wait()
        place_down(j)


def fused(n, unit_place, acts_slab, both_all, weight, down_slabs):
    tokens, slab = acts_slab.shape
    out_width = both_all.shape[2]
    rank = down_slabs.shape[1]
    rows = tokens // n
    unit_rows = rows // SLOTS
    vmem = pl.BlockSpec(memory_space=pltpu.VMEM)
    dma = pltpu.SemaphoreType.DMA((n,))
    return pl.pallas_call(
        functools.partial(fused_kernel, n, unit_rows),
        in_specs=[pl.BlockSpec(memory_space=pltpu.SMEM)] + [vmem] * 4,
        out_specs=[vmem] * 3,
        out_shape=[
            jax.ShapeDtypeStruct((rows, n * slab), BF16),
            jax.ShapeDtypeStruct((rank, n * slab), F32),
            jax.ShapeDtypeStruct((rank, out_width), F32),
        ],
        scratch_shapes=[
            pltpu.VMEM((n, unit_rows, SLOTS * rank), BF16),
            pltpu.VMEM((n, unit_rows, SLOTS * rank), BF16),
            pltpu.VMEM((unit_rows, SLOTS * rank), BF16),
            pltpu.VMEM((n, unit_rows, SLOTS * rank), BF16),
            pltpu.VMEM((n, rows, slab), BF16),
            pltpu.VMEM((n, rows, slab), BF16),
            pltpu.VMEM((tokens, n * rank), BF16),
            pltpu.VMEM((n, rank, slab), BF16),
            pltpu.VMEM((n, rank, slab), BF16),
        ] + [dma] * 8,
        compiler_params=pltpu.CompilerParams(
            collective_id=0, has_side_effects=True, vmem_limit_bytes=52 * 2**20),
        cost_estimate=pl.CostEstimate(
            flops=2 * tokens * slab * out_width * 4, bytes_accessed=30 * 2**20, transcendentals=0),
    )(unit_place, acts_slab, both_all, weight, down_slabs)


def shards(
    acts,
    output_gradient,
    frozen_weight_codes,
    weight_block_scale,
    adapter_down_weight,
    adapter_up_weight,
    token_adapter_index,
    adapter_position,
):
    token_rows, row_extent = acts.shape
    out_width = output_gradient.shape[1]
    rank = adapter_down_weight.shape[2]
    n = lax.axis_size("dp")
    me = lax.axis_index("dp")
    unit_rows = token_rows // SLOTS
    slab = row_extent // n
    tokens = token_rows * n
    unit_adapter = token_adapter_index.reshape(-1, unit_rows)[:, :1]
    every = jnp.arange(adapter_position.shape[0], dtype=jnp.int32)[None, :]
    unit_place = jnp.sum(jnp.where(unit_adapter == every, adapter_position[None, :], 0), axis=1)

    up_t = adapter_up_weight.transpose(0, 2, 1)
    down_t = adapter_down_weight.transpose(0, 2, 1)
    row_ids = me * slab + jnp.arange(slab, dtype=jnp.int32)
    scale_rows = weight_block_scale[row_ids // BLK]
    codes = frozen_weight_codes.astype(F32).reshape(slab, out_width // BLK, BLK)
    weight = (codes * scale_rows[:, :, None]).astype(BF16).reshape(slab, out_width)

    adapters = n * up_t.shape[0]
    if tokens * out_width <= 4 * 2**20 and slab % BLK == 0 and adapters == n:
        both = jnp.concatenate([output_gradient, up_t[0]], axis=0)
        both_all = lax.all_gather(both, "dp", axis=0, tiled=True).reshape(n, -1, out_width)
        acts_slab, down_slabs = exchange(n, acts, down_t[0])
        input_gradient, down_out, up_out = fused(
            n, unit_place, acts_slab, both_all, weight, down_slabs)
        return (
            input_gradient,
            down_out[None].transpose(0, 2, 1),
            up_out[None].transpose(0, 2, 1),
        )
    grads_all = lax.all_gather(output_gradient, "dp", axis=0, tiled=True)
    up_all = lax.all_gather(up_t, "dp", axis=0, tiled=True)
    down_slabs = lax.all_to_all(down_t, "dp", split_axis=2, concat_axis=0, tiled=True)
    acts_slab = lax.all_to_all(acts, "dp", split_axis=1, concat_axis=0, tiled=True)
    rows = 2 * token_rows
    whole = lambda *shape: pl.BlockSpec(shape, lambda i, place: (0,) * len(shape))
    out, proj_part, summed = pl.pallas_call(
        functools.partial(slab_kernel, unit_rows),
        grid_spec=pltpu.PrefetchScalarGridSpec(
            num_scalar_prefetch=1,
            grid=(tokens // rows,),
            in_specs=[
                pl.BlockSpec((rows, out_width), lambda i, place: (i, 0)),
                pl.BlockSpec((rows, slab), lambda i, place: (i, 0)),
                whole(slab, out_width),
                whole(adapters, rank, out_width),
                whole(adapters, rank, slab),
            ],
            out_specs=[
                pl.BlockSpec((rows, slab), lambda i, place: (i, 0)),
                pl.BlockSpec((rows, rank), lambda i, place: (i, 0)),
                whole(adapters, rank, slab),
            ],
        ),
        out_shape=[
            jax.ShapeDtypeStruct((tokens, slab), BF16),
            jax.ShapeDtypeStruct((tokens, rank), F32),
            jax.ShapeDtypeStruct((adapters, rank, slab), F32),
        ],
        compiler_params=pltpu.CompilerParams(vmem_limit_bytes=56 * 2**20),
    )(unit_place, grads_all, acts_slab, weight, up_all, down_slabs)

    proj_own = lax.psum_scatter(proj_part, "dp", scatter_dimension=0, tiled=True).astype(BF16)
    proj_all = lax.all_gather(proj_own, "dp", axis=0, tiled=True)
    input_gradient = lax.all_to_all(out, "dp", split_axis=0, concat_axis=1, tiled=True)
    down_gradient = lax.all_to_all(
        summed.astype(BF16), "dp", split_axis=0, concat_axis=2, tiled=True
    ).astype(F32)
    up_gradient = pl.pallas_call(
        up_kernel,
        grid_spec=pltpu.PrefetchScalarGridSpec(
            num_scalar_prefetch=2,
            grid=(tokens // unit_rows,),
            in_specs=[
                pl.BlockSpec((unit_rows, out_width), lambda i, place, me: (i, 0)),
                pl.BlockSpec((unit_rows, rank), lambda i, place, me: (i, 0)),
            ],
            out_specs=pl.BlockSpec((rank, out_width), lambda i, place, me: (0, 0)),
        ),
        out_shape=jax.ShapeDtypeStruct((rank, out_width), F32),
    )(unit_place, me.astype(jnp.int32).reshape(1), grads_all, proj_all)
    return (
        input_gradient,
        down_gradient.transpose(0, 2, 1),
        up_gradient[None].transpose(0, 2, 1),
    )


def solution(mesh):
    placed = (
        P(("groups", "dp"), None),
        P(("groups", "dp"), None),
        P("dp", None),
        P(),
        P("dp", None, None),
        P("dp", None, None),
        P("groups", None),
        P(),
    )
    return jax.shard_map(
        shards,
        mesh=mesh,
        in_specs=placed,
        out_specs=(
            P(("groups", "dp"), None),
            P(("groups", "dp"), None, None),
            P(("groups", "dp"), None, None),
        ),
        check_vma=False,
    )
```

```python
import functools

import jax
import jax.numpy as jnp
from jax import lax
from jax.experimental import pallas as pl
from jax.experimental.pallas import tpu as pltpu
from jax.sharding import PartitionSpec as P

BLK = 128
SLOTS = 2
PLANE = 4
NT = (((1,), (1,)), ((), ()))
TN = (((0,), (0,)), ((), ()))
F32 = jnp.float32
BF16 = jnp.bfloat16


def slab_kernel(unit_rows, place, grads, acts, weight, up, down, out, proj, summed):
    step = pl.program_id(0)

    @pl.when(step == 0)
    def _():
        summed[...] = jnp.zeros_like(summed)

    base = lax.dot_general(grads[...], weight[...], NT, preferred_element_type=F32)
    units = grads.shape[0] // unit_rows
    for u in range(units):
        rows = pl.ds(u * unit_rows, unit_rows)
        p = place[step * units + u]
        down_p = down[p]
        x = acts[rows, :]
        low = lax.dot_general(grads[rows, :], up[p], NT, preferred_element_type=F32).astype(BF16)
        proj[rows, :] = lax.dot_general(x, down_p, NT, preferred_element_type=F32)
        back = (0.5 * jnp.dot(low, down_p, preferred_element_type=F32)).astype(BF16)
        here = base[u * unit_rows : (u + 1) * unit_rows, :]
        out[rows, :] = (here + back.astype(F32)).astype(BF16)
        summed[p] += 0.5 * lax.dot_general(low, x, TN, preferred_element_type=F32)


def up_kernel(place_ref, me_ref, grads, proj, total):
    step = pl.program_id(0)
    unit_rows = grads.shape[0]

    @pl.when(step == 0)
    def _():
        total[...] = jnp.zeros_like(total)

    @pl.when(place_ref[step] == me_ref[0])
    def _():
        total[...] += 0.5 * lax.dot_general(
            proj[...], grads[...], TN, preferred_element_type=F32
        )


def exchange_kernel(n, acts, down, both, acts_out, down_out, gathered, acts_s, acts_r, down_s,
                    down_r, up_s, low_s, side_s, core_s, got_r, local):
    me = lax.axis_index("dp")
    rows = acts.shape[0]
    slab = acts.shape[1] // n

    def peer(s):
        return lax.rem(me + s, n)

    def cols(j):
        return pl.ds(pl.multiple_of(j * slab, slab), slab)

    def lines(j):
        return pl.ds(pl.multiple_of(j * rows, 16), rows)

    def remote(src, dst, send_sem, recv_sem, j):
        return pltpu.make_async_remote_copy(
            src_ref=src, dst_ref=dst, send_sem=send_sem, recv_sem=recv_sem,
            device_id={"dp": j}, device_id_type=pl.DeviceIdType.MESH)

    mine = pltpu.make_async_copy(acts.at[:, cols(me)], acts_out.at[lines(me), :], local.at[0])
    own = pltpu.make_async_copy(down.at[:, cols(me)], down_out.at[me], local.at[1])
    mine.start()
    own.start()
    first = pltpu.make_async_copy(both, gathered.at[me], local.at[2])
    first.start()
    barrier = pltpu.get_barrier_semaphore()

    @pl.loop(1, n)
    def _(s):
        pl.semaphore_signal(barrier, inc=1, device_id={"dp": peer(s)},
                            device_id_type=pl.DeviceIdType.MESH)

    pl.semaphore_wait(barrier, n - 1)
    first.wait()

    planes = n // PLANE
    z, q = lax.div(me, PLANE), lax.rem(me, PLANE)
    side_q = lax.rem(q + PLANE // 2, PLANE)
    core_q = q + 1 - 2 * lax.rem(q, 2)
    far_q = lax.rem(core_q + PLANE // 2, PLANE)
    side, core = z * PLANE + side_q, z * PLANE + core_q

    def hand(b, j, sems):
        return remote(gathered.at[b], gathered.at[b], sems.at[b], got_r.at[b], j)

    def spread(b, upward, downward):
        if upward:
            @pl.when(z + 1 < planes)
            def _():
                hand(b, me + PLANE, up_s).start()
        if downward:
            @pl.when(z >= 1)
            def _():
                hand(b, me - PLANE, low_s).start()
        hand(b, side, side_s).start()
        hand(b, core, core_s).start()

    def send_acts(lo, hi):
        @pl.loop(lo, hi)
        def _(s):
            j = peer(s)
            remote(acts.at[:, cols(j)], acts_out.at[lines(me), :], acts_s.at[j], acts_r.at[me],
                   j).start()

    spread(me, True, True)

    @pl.loop(1, n)
    def _(s):
        j = peer(s)
        remote(down.at[:, cols(j)], down_out.at[me], down_s.at[j], down_r.at[me], j).start()

    cuts = [1 + (n - 1) * k // planes for k in range(planes + 1)]
    send_acts(cuts[0], cuts[1])
    for k in range(1, planes):
        @pl.when(z >= k)
        def _():
            b = (z - k) * PLANE + q
            hand(b, core, core_s).wait_recv()
            spread(b, True, False)

        @pl.when(z + k < planes)
        def _():
            b = (z + k) * PLANE + q
            hand(b, core, core_s).wait_recv()
            spread(b, False, True)

        send_acts(cuts[k], cuts[k + 1])

    @pl.loop(0, planes)
    def _(zz):
        b = zz * PLANE + side_q
        hand(b, core, core_s).wait_recv()
        hand(b, core, core_s).start()

    @pl.loop(0, planes)
    def _(zz):
        hand(zz * PLANE + core_q, core, core_s).wait_recv()
        hand(zz * PLANE + far_q, core, core_s).wait_recv()
        hand(zz * PLANE + side_q, core, core_s).wait_send()
        b = zz * PLANE + q
        hand(b, core, core_s).wait_send()
        hand(b, side, side_s).wait_send()

        @pl.when((z + 1 < planes) & (zz <= z))
        def _():
            hand(b, me + PLANE, up_s).wait_send()

        @pl.when((z >= 1) & (zz >= z))
        def _():
            hand(b, me - PLANE, low_s).wait_send()

    mine.wait()
    own.wait()

    @pl.loop(1, n)
    def _(s):
        j = lax.rem(me + n - s, n)
        remote(down.at[:, cols(j)], down_out.at[j], down_s.at[j], down_r.at[j], j).wait()
        remote(acts.at[:, cols(j)], acts_out.at[lines(j), :], acts_s.at[j], acts_r.at[j],
               j).wait()


def exchange(n, acts, down_t, both):
    rows, width = acts.shape
    slab = width // n
    dma = pltpu.SemaphoreType.DMA((n,))
    anywhere = pl.BlockSpec(memory_space=pl.ANY)
    return pl.pallas_call(
        functools.partial(exchange_kernel, n),
        in_specs=[anywhere] * 3,
        out_specs=[anywhere] * 3,
        out_shape=[
            jax.ShapeDtypeStruct((n * rows, slab), BF16),
            jax.ShapeDtypeStruct((n, down_t.shape[0], slab), BF16),
            jax.ShapeDtypeStruct((n, *both.shape), BF16),
        ],
        scratch_shapes=[dma] * 9 + [pltpu.SemaphoreType.DMA((3,))],
        compiler_params=pltpu.CompilerParams(collective_id=1, has_side_effects=True),
        cost_estimate=pl.CostEstimate(
            flops=0, bytes_accessed=200 * 2**20, transcendentals=0),
    )(acts, down_t, both)


def fused_kernel(n, unit_rows, place, acts, both_all, weight, down, out, dgrad, ugrad,
                 part, part_in, own, projs, stage, landed, spread, dsend, dland,
                 part_s, part_r, proj_s, proj_r, out_s, out_r, down_s, down_r):
    me = lax.axis_index("dp")
    rows = SLOTS * unit_rows
    slab = weight.shape[0]
    rank = down.shape[1]
    wide = SLOTS * rank

    def peer(s):
        return lax.rem(me + s, n)

    def send(src, dst, send_sem, recv_sem, j):
        return pltpu.make_async_remote_copy(
            src_ref=src, dst_ref=dst, send_sem=send_sem.at[j], recv_sem=recv_sem.at[me],
            device_id={"dp": j}, device_id_type=pl.DeviceIdType.MESH)

    def arrival(src, dst, send_sem, recv_sem, j):
        return pltpu.make_async_remote_copy(
            src_ref=src, dst_ref=dst, send_sem=send_sem.at[j], recv_sem=recv_sem.at[j],
            device_id={"dp": j}, device_id_type=pl.DeviceIdType.MESH)

    barrier = pltpu.get_barrier_semaphore()

    @pl.loop(1, n)
    def _(s):
        pl.semaphore_signal(barrier, inc=1, device_id={"dp": peer(s)},
                            device_id_type=pl.DeviceIdType.MESH)

    pl.semaphore_wait(barrier, n - 1)

    def grad_tile(j, u):
        return both_all[j, pl.ds(u * unit_rows, unit_rows), :]

    def up_of(p):
        return both_all[p, pl.ds(rows, rank), :]

    def tile(j, u):
        return pl.ds(pl.multiple_of(j * rows + u * unit_rows, 16), unit_rows)

    def project(j, dst):
        both = [
            lax.dot_general(acts[tile(j, u), :], down[place[SLOTS * j + u]], NT,
                            preferred_element_type=F32)
            for u in range(SLOTS)
        ]
        dst[j] = jnp.concatenate(both, axis=1).astype(BF16)

    @pl.loop(1, n)
    def _(s):
        j = peer(s)
        project(j, part)
        send(part.at[j], part_in.at[me], part_s, part_r, j).start()

    project(me, part_in)

    lane_half = lax.broadcasted_iota(jnp.int32, (unit_rows, 2 * rank), 1) // rank

    def block(j, dst):
        for u in range(SLOTS):
            at = tile(j, u)
            p = place[SLOTS * j + u]
            g = grad_tile(j, u)
            low = lax.dot_general(g, up_of(p), NT, preferred_element_type=F32).astype(BF16)
            base = lax.dot_general(g, weight[...], NT, preferred_element_type=F32)
            back = (0.5 * jnp.dot(low, down[p], preferred_element_type=F32)).astype(BF16)
            dst[j, pl.ds(u * unit_rows, unit_rows), :] = (base + back.astype(F32)).astype(BF16)
            low = low.astype(F32)
            twice = jnp.concatenate([low, low], axis=1)
            for c in range(n // 2):
                kept = jnp.where(lane_half + 2 * c == p, twice, 0.0)
                spread[at, pl.ds(c * 2 * rank, 2 * rank)] = kept.astype(BF16)

    @pl.loop(1, n)
    def _(s):
        j = peer(s)
        block(j, stage)
        send(stage.at[j], landed.at[me], out_s, out_r, j).start()

    block(me, landed)

    @pl.loop(1, n)
    def _(s):
        j = peer(s)
        arrival(part.at[j], part_in.at[j], part_s, part_r, j).wait()

    total = part_in[0].astype(F32)
    for j in range(1, n):
        total = total + part_in[j].astype(F32)
    own[...] = total.astype(BF16)

    @pl.loop(1, n)
    def _(s):
        j = peer(s)
        send(own, projs.at[me], proj_s, proj_r, j).start()

    projs[me] = own[...]

    group = 4

    @pl.loop(0, n // group)
    def _(c):
        cols = pl.ds(pl.multiple_of(c * group * rank, group * rank), group * rank)
        got = 0.5 * lax.dot_general(spread[:, cols], acts[...], TN, preferred_element_type=F32)
        for i in range(group):
            dsend[c * group + i] = got[i * rank : (i + 1) * rank, :].astype(BF16)
        for i in range(group):
            j = c * group + i

            @pl.when(j != me)
            def _():
                send(dsend.at[j], dland.at[me], down_s, down_r, j).start()

    dland[me] = dsend[me]

    @pl.loop(1, n)
    def _(s):
        j = peer(s)
        arrival(own, projs.at[j], proj_s, proj_r, j).wait()

    ugrad[...] = jnp.zeros_like(ugrad)

    @pl.loop(0, n)
    def _(j):
        both = projs[j].astype(F32)
        for u in range(SLOTS):
            keep = jnp.where(place[SLOTS * j + u] == me, 0.5, 0.0)
            mine = (both[:, u * rank : (u + 1) * rank] * keep).astype(BF16)
            ugrad[...] += lax.dot_general(mine, grad_tile(j, u), TN,
                                          preferred_element_type=F32)

    def place_out(j):
        cols = pl.ds(pl.multiple_of(j * slab, slab), slab)
        out[:, cols] = landed[j]

    def place_down(j):
        cols = pl.ds(pl.multiple_of(j * slab, slab), slab)
        dgrad[:, cols] = dland[j].astype(F32)

    place_out(me)
    place_down(me)

    @pl.loop(1, n)
    def _(s):
        j = lax.rem(me + n - s, n)
        arrival(stage.at[j], landed.at[j], out_s, out_r, j).wait()
        place_out(j)

    @pl.loop(1, n)
    def _(s):
        j = lax.rem(me + n - s, n)
        arrival(dsend.at[j], dland.at[j], down_s, down_r, j).wait()
        place_down(j)


def fused(n, unit_place, acts_slab, both_all, weight, down_slabs):
    tokens, slab = acts_slab.shape
    out_width = both_all.shape[2]
    rank = down_slabs.shape[1]
    rows = tokens // n
    unit_rows = rows // SLOTS
    vmem = pl.BlockSpec(memory_space=pltpu.VMEM)
    dma = pltpu.SemaphoreType.DMA((n,))
    return pl.pallas_call(
        functools.partial(fused_kernel, n, unit_rows),
        in_specs=[pl.BlockSpec(memory_space=pltpu.SMEM)] + [vmem] * 4,
        out_specs=[vmem] * 3,
        out_shape=[
            jax.ShapeDtypeStruct((rows, n * slab), BF16),
            jax.ShapeDtypeStruct((rank, n * slab), F32),
            jax.ShapeDtypeStruct((rank, out_width), F32),
        ],
        scratch_shapes=[
            pltpu.VMEM((n, unit_rows, SLOTS * rank), BF16),
            pltpu.VMEM((n, unit_rows, SLOTS * rank), BF16),
            pltpu.VMEM((unit_rows, SLOTS * rank), BF16),
            pltpu.VMEM((n, unit_rows, SLOTS * rank), BF16),
            pltpu.VMEM((n, rows, slab), BF16),
            pltpu.VMEM((n, rows, slab), BF16),
            pltpu.VMEM((tokens, n * rank), BF16),
            pltpu.VMEM((n, rank, slab), BF16),
            pltpu.VMEM((n, rank, slab), BF16),
        ] + [dma] * 8,
        compiler_params=pltpu.CompilerParams(
            collective_id=0, has_side_effects=True, vmem_limit_bytes=52 * 2**20),
        cost_estimate=pl.CostEstimate(
            flops=2 * tokens * slab * out_width * 4, bytes_accessed=30 * 2**20, transcendentals=0),
    )(unit_place, acts_slab, both_all, weight, down_slabs)


def shards(
    acts,
    output_gradient,
    frozen_weight_codes,
    weight_block_scale,
    adapter_down_weight,
    adapter_up_weight,
    token_adapter_index,
    adapter_position,
):
    token_rows, row_extent = acts.shape
    out_width = output_gradient.shape[1]
    rank = adapter_down_weight.shape[2]
    n = lax.axis_size("dp")
    me = lax.axis_index("dp")
    unit_rows = token_rows // SLOTS
    slab = row_extent // n
    tokens = token_rows * n
    unit_adapter = token_adapter_index.reshape(-1, unit_rows)[:, :1]
    every = jnp.arange(adapter_position.shape[0], dtype=jnp.int32)[None, :]
    unit_place = jnp.sum(jnp.where(unit_adapter == every, adapter_position[None, :], 0), axis=1)

    up_t = adapter_up_weight.transpose(0, 2, 1)
    down_t = adapter_down_weight.transpose(0, 2, 1)
    row_ids = me * slab + jnp.arange(slab, dtype=jnp.int32)
    scale_rows = weight_block_scale[row_ids // BLK]
    codes = frozen_weight_codes.astype(F32).reshape(slab, out_width // BLK, BLK)
    weight = (codes * scale_rows[:, :, None]).astype(BF16).reshape(slab, out_width)

    adapters = n * up_t.shape[0]
    if tokens * out_width <= 4 * 2**20 and slab % BLK == 0 and adapters == n and n % PLANE == 0:
        both = jnp.concatenate([output_gradient, up_t[0]], axis=0)
        acts_slab, down_slabs, both_all = exchange(n, acts, down_t[0], both)
        input_gradient, down_out, up_out = fused(
            n, unit_place, acts_slab, both_all, weight, down_slabs)
        return (
            input_gradient,
            down_out[None].transpose(0, 2, 1),
            up_out[None].transpose(0, 2, 1),
        )
    grads_all = lax.all_gather(output_gradient, "dp", axis=0, tiled=True)
    up_all = lax.all_gather(up_t, "dp", axis=0, tiled=True)
    down_slabs = lax.all_to_all(down_t, "dp", split_axis=2, concat_axis=0, tiled=True)
    acts_slab = lax.all_to_all(acts, "dp", split_axis=1, concat_axis=0, tiled=True)
    rows = 2 * token_rows
    whole = lambda *shape: pl.BlockSpec(shape, lambda i, place: (0,) * len(shape))
    out, proj_part, summed = pl.pallas_call(
        functools.partial(slab_kernel, unit_rows),
        grid_spec=pltpu.PrefetchScalarGridSpec(
            num_scalar_prefetch=1,
            grid=(tokens // rows,),
            in_specs=[
                pl.BlockSpec((rows, out_width), lambda i, place: (i, 0)),
                pl.BlockSpec((rows, slab), lambda i, place: (i, 0)),
                whole(slab, out_width),
                whole(adapters, rank, out_width),
                whole(adapters, rank, slab),
            ],
            out_specs=[
                pl.BlockSpec((rows, slab), lambda i, place: (i, 0)),
                pl.BlockSpec((rows, rank), lambda i, place: (i, 0)),
                whole(adapters, rank, slab),
            ],
        ),
        out_shape=[
            jax.ShapeDtypeStruct((tokens, slab), BF16),
            jax.ShapeDtypeStruct((tokens, rank), F32),
            jax.ShapeDtypeStruct((adapters, rank, slab), F32),
        ],
        compiler_params=pltpu.CompilerParams(vmem_limit_bytes=56 * 2**20),
    )(unit_place, grads_all, acts_slab, weight, up_all, down_slabs)

    proj_own = lax.psum_scatter(proj_part, "dp", scatter_dimension=0, tiled=True).astype(BF16)
    proj_all = lax.all_gather(proj_own, "dp", axis=0, tiled=True)
    input_gradient = lax.all_to_all(out, "dp", split_axis=0, concat_axis=1, tiled=True)
    down_gradient = lax.all_to_all(
        summed.astype(BF16), "dp", split_axis=0, concat_axis=2, tiled=True
    ).astype(F32)
    up_gradient = pl.pallas_call(
        up_kernel,
        grid_spec=pltpu.PrefetchScalarGridSpec(
            num_scalar_prefetch=2,
            grid=(tokens // unit_rows,),
            in_specs=[
                pl.BlockSpec((unit_rows, out_width), lambda i, place, me: (i, 0)),
                pl.BlockSpec((unit_rows, rank), lambda i, place, me: (i, 0)),
            ],
            out_specs=pl.BlockSpec((rank, out_width), lambda i, place, me: (0, 0)),
        ),
        out_shape=jax.ShapeDtypeStruct((rank, out_width), F32),
    )(unit_place, me.astype(jnp.int32).reshape(1), grads_all, proj_all)
    return (
        input_gradient,
        down_gradient.transpose(0, 2, 1),
        up_gradient[None].transpose(0, 2, 1),
    )


def solution(mesh):
    placed = (
        P(("groups", "dp"), None),
        P(("groups", "dp"), None),
        P("dp", None),
        P(),
        P("dp", None, None),
        P("dp", None, None),
        P("groups", None),
        P(),
    )
    return jax.shard_map(
        shards,
        mesh=mesh,
        in_specs=placed,
        out_specs=(
            P(("groups", "dp"), None),
            P(("groups", "dp"), None, None),
            P(("groups", "dp"), None, None),
        ),
        check_vma=False,
    )
```

```python
import functools

import jax
import jax.numpy as jnp
from jax import lax
from jax.experimental import pallas as pl
from jax.experimental.pallas import tpu as pltpu
from jax.sharding import PartitionSpec as P

BLK = 128
SLOTS = 2
PLANE = 4
NT = (((1,), (1,)), ((), ()))
TN = (((0,), (0,)), ((), ()))
F32 = jnp.float32
BF16 = jnp.bfloat16


def slab_kernel(unit_rows, place, grads, acts, weight, up, down, out, proj, summed):
    step = pl.program_id(0)

    @pl.when(step == 0)
    def _():
        summed[...] = jnp.zeros_like(summed)

    base = lax.dot_general(grads[...], weight[...], NT, preferred_element_type=F32)
    units = grads.shape[0] // unit_rows
    for u in range(units):
        rows = pl.ds(u * unit_rows, unit_rows)
        p = place[step * units + u]
        down_p = down[p]
        x = acts[rows, :]
        low = lax.dot_general(grads[rows, :], up[p], NT, preferred_element_type=F32).astype(BF16)
        proj[rows, :] = lax.dot_general(x, down_p, NT, preferred_element_type=F32)
        back = (0.5 * jnp.dot(low, down_p, preferred_element_type=F32)).astype(BF16)
        here = base[u * unit_rows : (u + 1) * unit_rows, :]
        out[rows, :] = (here + back.astype(F32)).astype(BF16)
        summed[p] += 0.5 * lax.dot_general(low, x, TN, preferred_element_type=F32)


def up_kernel(place_ref, me_ref, grads, proj, total):
    step = pl.program_id(0)
    unit_rows = grads.shape[0]

    @pl.when(step == 0)
    def _():
        total[...] = jnp.zeros_like(total)

    @pl.when(place_ref[step] == me_ref[0])
    def _():
        total[...] += 0.5 * lax.dot_general(
            proj[...], grads[...], TN, preferred_element_type=F32
        )


def exchange_kernel(n, down, both, down_out, gathered, down_s, down_r, up_s, low_s, side_s, core_s, got_r, local):
    me = lax.axis_index("dp")
    slab = down.shape[1] // n

    def peer(s):
        return lax.rem(me + s, n)

    def cols(j):
        return pl.ds(pl.multiple_of(j * slab, slab), slab)

    def remote(src, dst, send_sem, recv_sem, j):
        return pltpu.make_async_remote_copy(
            src_ref=src, dst_ref=dst, send_sem=send_sem, recv_sem=recv_sem,
            device_id={"dp": j}, device_id_type=pl.DeviceIdType.MESH)

    own = pltpu.make_async_copy(down.at[:, cols(me)], down_out.at[me], local.at[1])
    own.start()
    first = pltpu.make_async_copy(both, gathered.at[me], local.at[2])
    first.start()
    barrier = pltpu.get_barrier_semaphore()

    @pl.loop(1, n)
    def _(s):
        pl.semaphore_signal(barrier, inc=1, device_id={"dp": peer(s)},
                            device_id_type=pl.DeviceIdType.MESH)

    pl.semaphore_wait(barrier, n - 1)
    first.wait()

    planes = n // PLANE
    z, q = lax.div(me, PLANE), lax.rem(me, PLANE)
    side_q = lax.rem(q + PLANE // 2, PLANE)
    core_q = q + 1 - 2 * lax.rem(q, 2)
    far_q = lax.rem(core_q + PLANE // 2, PLANE)
    side, core = z * PLANE + side_q, z * PLANE + core_q

    def hand(b, j, sems):
        return remote(gathered.at[b], gathered.at[b], sems.at[b], got_r.at[b], j)

    def spread(b, upward, downward):
        if upward:
            @pl.when(z + 1 < planes)
            def _():
                hand(b, me + PLANE, up_s).start()
        if downward:
            @pl.when(z >= 1)
            def _():
                hand(b, me - PLANE, low_s).start()
        hand(b, side, side_s).start()
        hand(b, core, core_s).start()

    spread(me, True, True)

    @pl.loop(1, n)
    def _(s):
        j = peer(s)
        remote(down.at[:, cols(j)], down_out.at[me], down_s.at[j], down_r.at[me], j).start()

    for k in range(1, planes):
        @pl.when(z >= k)
        def _():
            b = (z - k) * PLANE + q
            hand(b, core, core_s).wait_recv()
            spread(b, True, False)

        @pl.when(z + k < planes)
        def _():
            b = (z + k) * PLANE + q
            hand(b, core, core_s).wait_recv()
            spread(b, False, True)

    @pl.loop(0, planes)
    def _(zz):
        b = zz * PLANE + side_q
        hand(b, core, core_s).wait_recv()
        hand(b, core, core_s).start()

    @pl.loop(0, planes)
    def _(zz):
        hand(zz * PLANE + core_q, core, core_s).wait_recv()
        hand(zz * PLANE + far_q, core, core_s).wait_recv()
        hand(zz * PLANE + side_q, core, core_s).wait_send()
        b = zz * PLANE + q
        hand(b, core, core_s).wait_send()
        hand(b, side, side_s).wait_send()

        @pl.when((z + 1 < planes) & (zz <= z))
        def _():
            hand(b, me + PLANE, up_s).wait_send()

        @pl.when((z >= 1) & (zz >= z))
        def _():
            hand(b, me - PLANE, low_s).wait_send()

    own.wait()

    @pl.loop(1, n)
    def _(s):
        j = lax.rem(me + n - s, n)
        remote(down.at[:, cols(j)], down_out.at[j], down_s.at[j], down_r.at[j], j).wait()


def exchange(n, down_t, both):
    slab = down_t.shape[1] // n
    dma = pltpu.SemaphoreType.DMA((n,))
    anywhere = pl.BlockSpec(memory_space=pl.ANY)
    return pl.pallas_call(
        functools.partial(exchange_kernel, n),
        in_specs=[anywhere] * 2,
        out_specs=[anywhere] * 2,
        out_shape=[
            jax.ShapeDtypeStruct((n, down_t.shape[0], slab), BF16),
            jax.ShapeDtypeStruct((n, *both.shape), BF16),
        ],
        scratch_shapes=[dma] * 7 + [pltpu.SemaphoreType.DMA((3,))],
        compiler_params=pltpu.CompilerParams(collective_id=1, has_side_effects=True),
        cost_estimate=pl.CostEstimate(
            flops=0, bytes_accessed=200 * 2**20, transcendentals=0),
    )(down_t, both)


def fused_kernel(n, unit_rows, place, acts_own, both_all, weight, down, out, dgrad, ugrad,
                 acts, part, part_in, own, projs, stage, landed, spread, dsend, dland,
                 part_s, part_r, proj_s, proj_r, out_s, out_r, down_s, down_r,
                 acts_s, acts_r, local):
    me = lax.axis_index("dp")
    rows = SLOTS * unit_rows
    slab = weight.shape[0]
    rank = down.shape[1]
    wide = SLOTS * rank

    def peer(s):
        return lax.rem(me + s, n)

    def send(src, dst, send_sem, recv_sem, j):
        return pltpu.make_async_remote_copy(
            src_ref=src, dst_ref=dst, send_sem=send_sem.at[j], recv_sem=recv_sem.at[me],
            device_id={"dp": j}, device_id_type=pl.DeviceIdType.MESH)

    def arrival(src, dst, send_sem, recv_sem, j):
        return pltpu.make_async_remote_copy(
            src_ref=src, dst_ref=dst, send_sem=send_sem.at[j], recv_sem=recv_sem.at[j],
            device_id={"dp": j}, device_id_type=pl.DeviceIdType.MESH)

    barrier = pltpu.get_barrier_semaphore()

    @pl.loop(1, n)
    def _(s):
        pl.semaphore_signal(barrier, inc=1, device_id={"dp": peer(s)},
                            device_id_type=pl.DeviceIdType.MESH)

    pl.semaphore_wait(barrier, n - 1)

    def grad_tile(j, u):
        return both_all[j, pl.ds(u * unit_rows, unit_rows), :]

    def up_of(p):
        return both_all[p, pl.ds(rows, rank), :]

    def tile(j, u):
        return pl.ds(pl.multiple_of(j * rows + u * unit_rows, 16), unit_rows)

    def project(j, dst):
        both = [
            lax.dot_general(acts[tile(j, u), :], down[place[SLOTS * j + u]], NT,
                            preferred_element_type=F32)
            for u in range(SLOTS)
        ]
        dst[j] = jnp.concatenate(both, axis=1).astype(BF16)

    def acts_cols(j):
        return acts_own.at[:, pl.ds(pl.multiple_of(j * slab, slab), slab)]

    def acts_rows(j):
        return acts.at[pl.ds(pl.multiple_of(j * rows, 16), rows), :]

    mine = pltpu.make_async_copy(acts_cols(me), acts_rows(me), local.at[0])
    mine.start()

    @pl.loop(1, n)
    def _(s):
        j = peer(s)
        send(acts_cols(j), acts_rows(me), acts_s, acts_r, j).start()

    lane_half = lax.broadcasted_iota(jnp.int32, (unit_rows, 2 * rank), 1) // rank

    def block(j, dst):
        for u in range(SLOTS):
            at = tile(j, u)
            p = place[SLOTS * j + u]
            g = grad_tile(j, u)
            low = lax.dot_general(g, up_of(p), NT, preferred_element_type=F32).astype(BF16)
            base = lax.dot_general(g, weight[...], NT, preferred_element_type=F32)
            back = (0.5 * jnp.dot(low, down[p], preferred_element_type=F32)).astype(BF16)
            dst[j, pl.ds(u * unit_rows, unit_rows), :] = (base + back.astype(F32)).astype(BF16)
            low = low.astype(F32)
            twice = jnp.concatenate([low, low], axis=1)
            for c in range(n // 2):
                kept = jnp.where(lane_half + 2 * c == p, twice, 0.0)
                spread[at, pl.ds(c * 2 * rank, 2 * rank)] = kept.astype(BF16)

    @pl.loop(1, n)
    def _(s):
        j = peer(s)
        block(j, stage)
        send(stage.at[j], landed.at[me], out_s, out_r, j).start()

    block(me, landed)

    mine.wait()

    @pl.loop(1, n)
    def _(s):
        j = lax.rem(me + n - s, n)
        arrival(acts_cols(j), acts_rows(j), acts_s, acts_r, j).wait_recv()
        project(j, part)
        send(part.at[j], part_in.at[me], part_s, part_r, j).start()

    project(me, part_in)

    group = 4

    @pl.loop(0, n // group)
    def _(c):
        cols = pl.ds(pl.multiple_of(c * group * rank, group * rank), group * rank)
        got = 0.5 * lax.dot_general(spread[:, cols], acts[...], TN, preferred_element_type=F32)
        for i in range(group):
            dsend[c * group + i] = got[i * rank : (i + 1) * rank, :].astype(BF16)
        for i in range(group):
            j = c * group + i

            @pl.when(j != me)
            def _():
                send(dsend.at[j], dland.at[me], down_s, down_r, j).start()

    dland[me] = dsend[me]

    @pl.loop(1, n)
    def _(s):
        j = peer(s)
        arrival(part.at[j], part_in.at[j], part_s, part_r, j).wait()

    total = part_in[0].astype(F32)
    for j in range(1, n):
        total = total + part_in[j].astype(F32)
    own[...] = total.astype(BF16)

    @pl.loop(1, n)
    def _(s):
        j = peer(s)
        send(own, projs.at[me], proj_s, proj_r, j).start()

    projs[me] = own[...]

    @pl.loop(1, n)
    def _(s):
        j = peer(s)
        arrival(own, projs.at[j], proj_s, proj_r, j).wait()

    ugrad[...] = jnp.zeros_like(ugrad)

    @pl.loop(0, n)
    def _(j):
        both = projs[j].astype(F32)
        for u in range(SLOTS):
            keep = jnp.where(place[SLOTS * j + u] == me, 0.5, 0.0)
            mine = (both[:, u * rank : (u + 1) * rank] * keep).astype(BF16)
            ugrad[...] += lax.dot_general(mine, grad_tile(j, u), TN,
                                          preferred_element_type=F32)

    def place_out(j):
        cols = pl.ds(pl.multiple_of(j * slab, slab), slab)
        out[:, cols] = landed[j]

    def place_down(j):
        cols = pl.ds(pl.multiple_of(j * slab, slab), slab)
        dgrad[:, cols] = dland[j].astype(F32)

    place_out(me)
    place_down(me)

    @pl.loop(1, n)
    def _(s):
        j = lax.rem(me + n - s, n)
        arrival(acts_cols(j), acts_rows(j), acts_s, acts_r, j).wait_send()
        arrival(stage.at[j], landed.at[j], out_s, out_r, j).wait()
        place_out(j)

    @pl.loop(1, n)
    def _(s):
        j = lax.rem(me + n - s, n)
        arrival(dsend.at[j], dland.at[j], down_s, down_r, j).wait()
        place_down(j)


def fused(n, unit_place, acts, both_all, weight, down_slabs):
    slab = acts.shape[1] // n
    tokens = acts.shape[0] * n
    out_width = both_all.shape[2]
    rank = down_slabs.shape[1]
    rows = tokens // n
    unit_rows = rows // SLOTS
    vmem = pl.BlockSpec(memory_space=pltpu.VMEM)
    dma = pltpu.SemaphoreType.DMA((n,))
    return pl.pallas_call(
        functools.partial(fused_kernel, n, unit_rows),
        in_specs=[pl.BlockSpec(memory_space=pltpu.SMEM), pl.BlockSpec(memory_space=pl.ANY)]
        + [vmem] * 3,
        out_specs=[vmem] * 3,
        out_shape=[
            jax.ShapeDtypeStruct((rows, n * slab), BF16),
            jax.ShapeDtypeStruct((rank, n * slab), F32),
            jax.ShapeDtypeStruct((rank, out_width), F32),
        ],
        scratch_shapes=[
            pltpu.VMEM((tokens, slab), BF16),
            pltpu.VMEM((n, unit_rows, SLOTS * rank), BF16),
            pltpu.VMEM((n, unit_rows, SLOTS * rank), BF16),
            pltpu.VMEM((unit_rows, SLOTS * rank), BF16),
            pltpu.VMEM((n, unit_rows, SLOTS * rank), BF16),
            pltpu.VMEM((n, rows, slab), BF16),
            pltpu.VMEM((n, rows, slab), BF16),
            pltpu.VMEM((tokens, n * rank), BF16),
            pltpu.VMEM((n, rank, slab), BF16),
            pltpu.VMEM((n, rank, slab), BF16),
        ] + [dma] * 10 + [pltpu.SemaphoreType.DMA((1,))],
        compiler_params=pltpu.CompilerParams(
            collective_id=0, has_side_effects=True, vmem_limit_bytes=52 * 2**20),
        cost_estimate=pl.CostEstimate(
            flops=2 * tokens * slab * out_width * 4, bytes_accessed=30 * 2**20, transcendentals=0),
    )(unit_place, acts, both_all, weight, down_slabs)


def shards(
    acts,
    output_gradient,
    frozen_weight_codes,
    weight_block_scale,
    adapter_down_weight,
    adapter_up_weight,
    token_adapter_index,
    adapter_position,
):
    token_rows, row_extent = acts.shape
    out_width = output_gradient.shape[1]
    rank = adapter_down_weight.shape[2]
    n = lax.axis_size("dp")
    me = lax.axis_index("dp")
    unit_rows = token_rows // SLOTS
    slab = row_extent // n
    tokens = token_rows * n
    unit_adapter = token_adapter_index.reshape(-1, unit_rows)[:, :1]
    every = jnp.arange(adapter_position.shape[0], dtype=jnp.int32)[None, :]
    unit_place = jnp.sum(jnp.where(unit_adapter == every, adapter_position[None, :], 0), axis=1)

    up_t = adapter_up_weight.transpose(0, 2, 1)
    down_t = adapter_down_weight.transpose(0, 2, 1)
    row_ids = me * slab + jnp.arange(slab, dtype=jnp.int32)
    scale_rows = weight_block_scale[row_ids // BLK]
    codes = frozen_weight_codes.astype(F32).reshape(slab, out_width // BLK, BLK)
    weight = (codes * scale_rows[:, :, None]).astype(BF16).reshape(slab, out_width)

    adapters = n * up_t.shape[0]
    if tokens * out_width <= 4 * 2**20 and slab % BLK == 0 and adapters == n and n % PLANE == 0:
        both = jnp.concatenate([output_gradient, up_t[0]], axis=0)
        down_slabs, both_all = exchange(n, down_t[0], both)
        input_gradient, down_out, up_out = fused(
            n, unit_place, acts, both_all, weight, down_slabs)
        return (
            input_gradient,
            down_out[None].transpose(0, 2, 1),
            up_out[None].transpose(0, 2, 1),
        )
    grads_all = lax.all_gather(output_gradient, "dp", axis=0, tiled=True)
    up_all = lax.all_gather(up_t, "dp", axis=0, tiled=True)
    down_slabs = lax.all_to_all(down_t, "dp", split_axis=2, concat_axis=0, tiled=True)
    acts_slab = lax.all_to_all(acts, "dp", split_axis=1, concat_axis=0, tiled=True)
    rows = 2 * token_rows
    whole = lambda *shape: pl.BlockSpec(shape, lambda i, place: (0,) * len(shape))
    out, proj_part, summed = pl.pallas_call(
        functools.partial(slab_kernel, unit_rows),
        grid_spec=pltpu.PrefetchScalarGridSpec(
            num_scalar_prefetch=1,
            grid=(tokens // rows,),
            in_specs=[
                pl.BlockSpec((rows, out_width), lambda i, place: (i, 0)),
                pl.BlockSpec((rows, slab), lambda i, place: (i, 0)),
                whole(slab, out_width),
                whole(adapters, rank, out_width),
                whole(adapters, rank, slab),
            ],
            out_specs=[
                pl.BlockSpec((rows, slab), lambda i, place: (i, 0)),
                pl.BlockSpec((rows, rank), lambda i, place: (i, 0)),
                whole(adapters, rank, slab),
            ],
        ),
        out_shape=[
            jax.ShapeDtypeStruct((tokens, slab), BF16),
            jax.ShapeDtypeStruct((tokens, rank), F32),
            jax.ShapeDtypeStruct((adapters, rank, slab), F32),
        ],
        compiler_params=pltpu.CompilerParams(vmem_limit_bytes=56 * 2**20),
    )(unit_place, grads_all, acts_slab, weight, up_all, down_slabs)

    proj_own = lax.psum_scatter(proj_part, "dp", scatter_dimension=0, tiled=True).astype(BF16)
    proj_all = lax.all_gather(proj_own, "dp", axis=0, tiled=True)
    input_gradient = lax.all_to_all(out, "dp", split_axis=0, concat_axis=1, tiled=True)
    down_gradient = lax.all_to_all(
        summed.astype(BF16), "dp", split_axis=0, concat_axis=2, tiled=True
    ).astype(F32)
    up_gradient = pl.pallas_call(
        up_kernel,
        grid_spec=pltpu.PrefetchScalarGridSpec(
            num_scalar_prefetch=2,
            grid=(tokens // unit_rows,),
            in_specs=[
                pl.BlockSpec((unit_rows, out_width), lambda i, place, me: (i, 0)),
                pl.BlockSpec((unit_rows, rank), lambda i, place, me: (i, 0)),
            ],
            out_specs=pl.BlockSpec((rank, out_width), lambda i, place, me: (0, 0)),
        ),
        out_shape=jax.ShapeDtypeStruct((rank, out_width), F32),
    )(unit_place, me.astype(jnp.int32).reshape(1), grads_all, proj_all)
    return (
        input_gradient,
        down_gradient.transpose(0, 2, 1),
        up_gradient[None].transpose(0, 2, 1),
    )


def solution(mesh):
    placed = (
        P(("groups", "dp"), None),
        P(("groups", "dp"), None),
        P("dp", None),
        P(),
        P("dp", None, None),
        P("dp", None, None),
        P("groups", None),
        P(),
    )
    return jax.shard_map(
        shards,
        mesh=mesh,
        in_specs=placed,
        out_specs=(
            P(("groups", "dp"), None),
            P(("groups", "dp"), None, None),
            P(("groups", "dp"), None, None),
        ),
        check_vma=False,
    )
```
